32 devices in a mesh: store: 4 (over y, x), mod: 8 (over z, core).
Axes of the slice: x: 2, y: 2, z: 4, core: 2. Of those that a mesh axis runs over, the one named last changes fastest.
Arguments:
- act_proj: bfloat16 [256, 256, 512], P(('store', 'mod')), may hold values from -1.5 to 1.5
- grad_proj: bfloat16 [256, 256, 512], P(('store', 'mod')), may hold values from -1.5 to 1.5
- token_mask: int32 [256, 256], P(('store', 'mod')), may hold values 0 or 1
- layer_of: int32 [16], P('mod'), may hold values from 0 to 3, as said below
- layer_weight: float32 [4], replicated, may hold values from 0.25 to 4
- fisher_inv: bfloat16 [16, 1024, 1024], P('mod'), may hold values from -0.2 to 1.8
- stored_grads: bfloat16 [16384, 16384], P('store', 'mod'), may hold values from -0.049804688 to 0.049804688
Outputs:
- scores: float32 [256, 16384], P('mod', 'store')
The draws below stay inside these ranges and needn't reach their ends.
Inputs may be any that keep to these rules, and one draw needn't show every extreme that they name: `layer_of`: each of the 4 layers holds the same number of modules.
All inputs are finite; a program needn't handle non-finite values. No bound on the sum of `token_mask` on one device may be relied on, other than what follows from the above.
Results may differ from the reference program's by a relative error of at most 0.004.
Values may be sent and summed in bfloat16 or wider, within the bound.
A program may use at most 128 MiB of HBM per device.

```python
import math
import jax
import jax.numpy as jnp
from jax import lax

R = 32
RR = 1024
LEN = 256
MODS = 16
LAYERS = 4
Q = 256
NSTORE = 16384


def draw_layer_of(key, part):
    order = jax.random.permutation(key, jnp.arange(MODS, dtype=jnp.int32))
    return (order % LAYERS).astype(jnp.int32)


def draw_fisher_inv(key, part):
    key_off = jax.random.fold_in(key, 11)
    key_diag = jax.random.fold_in(key, 23)
    spread = 0.5 / math.sqrt(RR)
    off_part = jax.random.normal(key_off, (MODS, RR, RR), jnp.float32) * spread
    off_part = (off_part + jnp.swapaxes(off_part, 1, 2)) / math.sqrt(2.0)
    off_part = jnp.clip(off_part, -0.15, 0.15)
    diag_part = jax.random.uniform(key_diag, (MODS, RR), jnp.float32, 0.8, 1.6)
    ident = jnp.eye(RR, dtype=jnp.float32)
    return (off_part + diag_part[:, :, None] * ident[None, :, :]).astype(jnp.bfloat16)


def plant(drawn, own_key, smallest, top_value):
    extent = drawn.shape
    spot = [jax.random.randint(jax.random.fold_in(own_key, axis), (), 0, extent[axis]) for axis in range(len(extent))]
    drawn = drawn.at[tuple(spot)].set(smallest)
    longest = extent.index(max(extent))
    spot[longest] = (spot[longest] + 1) % extent[longest]
    return drawn.at[tuple(spot)].set(top_value)


def level_of(rng, extent, pieces, smallest, largest):
    factor_of = 1.0
    for axis_at, parts in pieces:
        steps = jax.random.uniform(jax.random.fold_in(jax.random.fold_in(rng, 6), axis_at), (parts,), jnp.float32, smallest / len(pieces), largest / len(pieces))
        factor_of = factor_of * jnp.repeat(jnp.exp(steps), extent[axis_at] // parts).reshape((-1,) + (1,) * (len(extent) - 1 - axis_at))
    return factor_of


def gaussian(stream_key, dims, scale, limit, shards=(), kind=jnp.bfloat16):
    loudness = level_of(stream_key, dims, shards, -0.22, 0.18) if shards else 1.0
    entries = jax.random.normal(stream_key, dims, jnp.float32) * scale * loudness
    return jnp.minimum(jnp.maximum(entries, -limit), limit).astype(kind)


def setup_inputs(seed: int = 0) -> dict:
    splits = jax.random.split(jax.random.key(seed), 8)
    act_proj = gaussian(splits[0], (Q, LEN, MODS * R), 0.25, 1.5, ((0, 32),))
    grad_proj = gaussian(splits[1], (Q, LEN, MODS * R), 0.25, 1.5, ((0, 32),))
    token_mask = plant((jax.random.randint(splits[2], (Q, LEN), 0, 4) < 3).astype(jnp.int32), jax.random.fold_in(splits[2], 1), 0, 1)
    layer_of = draw_layer_of(jax.random.fold_in(splits[7], 71), 0)
    layer_weight = jnp.clip(jnp.exp(jax.random.uniform(splits[4], (LAYERS,), jnp.float32, math.log(0.25), math.log(4.0))), 0.25, 4.0)
    fisher_inv = draw_fisher_inv(jax.random.fold_in(splits[7], 71), 0)
    stored_grads = gaussian(splits[6], (NSTORE, MODS * RR), 0.0078125, 0.049804688, ((0, 4), (1, 8)))
    return dict(act_proj=act_proj, grad_proj=grad_proj, token_mask=token_mask, layer_of=layer_of, layer_weight=layer_weight, fisher_inv=fisher_inv, stored_grads=stored_grads)


def reference(act_proj, grad_proj, token_mask, layer_of, layer_weight, fisher_inv, stored_grads):
    valid_mask = token_mask.astype(jnp.bfloat16)[:, :, None]
    grad_side = (grad_proj * valid_mask).reshape(Q, LEN, MODS, R)
    act_side = act_proj.reshape(Q, LEN, MODS, R)

    def one_query(pair):
        grad_one, act_one = pair
        outer = jnp.einsum("tmi,tmj->mij", grad_one.astype(jnp.float32), act_one.astype(jnp.float32))
        return outer.reshape(MODS, R * R)

    per_sample = lax.map(one_query, (grad_side, act_side)).astype(jnp.bfloat16)
    picked = layer_of[:, None] == jnp.arange(LAYERS, dtype=jnp.int32)[None, :]
    module_weight = jnp.sum(jnp.where(picked, layer_weight[None, :], jnp.zeros_like(layer_weight)[None, :]), axis=1)
    conditioned = jnp.einsum("qkr,krc->qkc", per_sample.astype(jnp.float32), fisher_inv.astype(jnp.float32))
    conditioned = (conditioned * module_weight[None, :, None]).astype(jnp.bfloat16)
    return jnp.dot(conditioned.reshape(Q, MODS * RR), stored_grads.T, preferred_element_type=jnp.float32)
```

```python
import functools

import jax
import jax.numpy as jnp
from jax import lax
from jax.experimental import pallas as pl
from jax.experimental.pallas import tpu as pltpu
from jax.sharding import PartitionSpec as P

R = 32
MESH = pl.DeviceIdType.MESH


def peer(index, step, count):
    if count & (count - 1):
        return lax.rem(index + step, count)
    other, bit = 0, 1
    while bit < count:
        other = other + ((index // bit + step // bit) % 2) * bit
        bit *= 2
    return other


def kernel(
    n_store, n_mod, width,
    send_ref, layer_ref, weight_ref, fisher_hbm, stored_hbm, out_ref,
    fisher, stored, blocks, everyone, keep, pair_out, pair_in, far_out, far_in,
    fisher_sem, stored_sem, block_send, block_recv, all_send, all_recv,
    pair_send, pair_recv, far_send, far_recv,
):
    s, k = lax.axis_index("store"), lax.axis_index("mod")
    chips = n_mod // 2
    chip, core = k // 2, k % 2
    sibling = k + 1 - 2 * core
    mods, entries = fisher.shape[0], fisher.shape[1]
    owned = out_ref.shape[0]
    samples = stored.shape[0]
    n_chunks = samples // width
    rows = everyone.shape[1]
    q_local = send_ref.shape[1] // mods

    fisher_copy = pltpu.make_async_copy(fisher_hbm, fisher, fisher_sem)
    fisher_copy.start()

    def stored_copy(c):
        part = pl.ds(pl.multiple_of(c * width, width), width)
        return pltpu.make_async_copy(stored_hbm.at[part, :], stored.at[part, :], stored_sem.at[c])

    for c in range(n_chunks):
        stored_copy(c).start()

    barrier = pltpu.get_barrier_semaphore()
    for d in range(1, n_mod):
        pl.semaphore_signal(barrier, inc=1, device_id=(s, peer(k, d, n_mod)), device_id_type=MESH)
    for d in range(1, n_store):
        pl.semaphore_signal(barrier, inc=1, device_id=(peer(s, d, n_store), k), device_id_type=MESH)
    pl.semaphore_wait(barrier, n_mod + n_store - 2)

    block_copies = []
    for d in range(n_mod - 1, 0, -1):
        to = peer(k, d, n_mod)
        copy = pltpu.make_async_remote_copy(
            src_ref=send_ref.at[to], dst_ref=blocks.at[k],
            send_sem=block_send.at[to], recv_sem=block_recv.at[k],
            device_id=(s, to), device_id_type=MESH,
        )
        copy.start()
        block_copies.append(copy)
    blocks[k] = send_ref[k]
    fisher_copy.wait()
    for d in range(1, n_mod):
        source = peer(k, d, n_mod)
        pltpu.make_async_remote_copy(
            src_ref=send_ref.at[source], dst_ref=blocks.at[source],
            send_sem=block_send.at[source], recv_sem=block_recv.at[source],
            device_id=(s, source), device_id_type=MESH,
        ).wait_recv()

    arrived = blocks[...].astype(jnp.float32).reshape(n_mod, mods, q_local, entries)
    for m in range(mods):
        layer = layer_ref[m]
        scale = jnp.float32(0.0)
        for at in range(weight_ref.shape[0]):
            scale = scale + jnp.where(layer == at, weight_ref[at], jnp.float32(0.0))
        mine = arrived[:, m].reshape(n_mod * q_local, entries).astype(jnp.bfloat16)
        product = jnp.dot(mine, fisher[m], preferred_element_type=jnp.float32)
        everyone[s, :, m * entries:(m + 1) * entries] = (product * scale).astype(jnp.bfloat16)

    all_copies = []
    for d in range(1, n_store):
        to = peer(s, d, n_store)
        copy = pltpu.make_async_remote_copy(
            src_ref=everyone.at[s], dst_ref=everyone.at[s],
            send_sem=all_send.at[to], recv_sem=all_recv.at[s],
            device_id=(to, k), device_id_type=MESH,
        )
        copy.start()
        all_copies.append(copy)

    def span(c):
        return pl.ds(pl.multiple_of(c * width, width), width)

    def pair_copy(j, c):
        return pltpu.make_async_remote_copy(
            src_ref=pair_out.at[j, c], dst_ref=pair_in.at[j, c],
            send_sem=pair_send.at[j, c], recv_sem=pair_recv.at[j, c],
            device_id=(s, sibling), device_id_type=MESH,
        )

    def far_copy(j, c):
        return pltpu.make_async_remote_copy(
            src_ref=far_out.at[j, c], dst_ref=far_in.at[chip, c],
            send_sem=far_send.at[j, c], recv_sem=far_recv.at[chip, c],
            device_id=(s, 2 * j + core), device_id_type=MESH,
        )

    def far_arrival(source, c):
        return pltpu.make_async_remote_copy(
            src_ref=far_out.at[source, c], dst_ref=far_in.at[source, c],
            send_sem=far_send.at[source, c], recv_sem=far_recv.at[source, c],
            device_id=(s, 2 * source + core), device_id_type=MESH,
        )

    def finish_pair(step):
        j, c = peer(s, step // n_chunks, n_store), step % n_chunks
        pair_copy(j, c).wait_recv()
        total = keep[j, c] + pair_in[j, c].astype(jnp.float32)

        @pl.when(j == chip)
        def _():
            out_ref[:, span(c)] = total

        @pl.when(j != chip)
        def _():
            far_out[j, c] = total.astype(jnp.bfloat16)
            far_copy(j, c).start()

    def score_step(step, carry):
        t, c = step // n_chunks, step % n_chunks
        j = peer(s, t, n_store)

        @pl.when((c == 0) & (t > 0))
        def _():
            pltpu.make_async_remote_copy(
                src_ref=everyone.at[j], dst_ref=everyone.at[j],
                send_sem=all_send.at[j], recv_sem=all_recv.at[j],
                device_id=(j, k), device_id_type=MESH,
            ).wait_recv()

        @pl.when(t == 0)
        def _():
            stored_copy(c).wait()

        part = lax.dot_general(
            everyone[j], stored[span(c), :], (((1,), (1,)), ((), ())), preferred_element_type=jnp.float32
        )
        low, high = part[:owned], part[owned:]
        first = core == 0
        keep[j, c] = jnp.where(first, low, high)
        pair_out[j, c] = jnp.where(first, high, low).astype(jnp.bfloat16)
        pair_copy(j, c).start()

        @pl.when(step > 0)
        def _():
            finish_pair(step - 1)

        return carry

    steps = n_store * n_chunks
    lax.fori_loop(0, steps, score_step, 0)
    finish_pair(steps - 1)

    for d in range(1, chips):
        source = peer(chip, d, chips)
        for c in range(n_chunks):
            far_arrival(source, c).wait_recv()
            out_ref[:, c * width:(c + 1) * width] += far_in[source, c].astype(jnp.float32)

    for copy in block_copies + all_copies:
        copy.wait_send()
    for j in range(chips):
        for c in range(n_chunks):
            pair_copy(j, c).wait_send()

            @pl.when(j != chip)
            def _():
                far_copy(j, c).wait_send()


def local(n_store, n_mod, act_proj, grad_proj, token_mask, layer_of, layer_weight, fisher_inv, stored_grads):
    q_local, length, columns = act_proj.shape
    modules = columns // R
    mods = modules // n_mod
    valid_mask = token_mask.astype(jnp.bfloat16)[:, :, None]
    grad_side = (grad_proj * valid_mask).reshape(q_local, length, modules, R)
    act_side = act_proj.reshape(q_local, length, modules, R)
    per_sample = jnp.einsum(
        "qtmi,qtmj->qmij", grad_side, act_side, preferred_element_type=jnp.float32
    )
    per_sample = per_sample.reshape(q_local, n_mod, mods, R * R).astype(jnp.bfloat16)
    to_send = per_sample.transpose(1, 2, 0, 3).reshape(n_mod, mods * q_local, R * R)
    samples, depth = stored_grads.shape
    queries = q_local * n_store * n_mod
    owned, rows, chips = queries // n_mod, queries // n_store, n_mod // 2
    assert rows == 2 * owned and chips == n_store
    width = min(1024, samples)
    n_chunks = samples // width
    bf16, f32 = jnp.bfloat16, jnp.float32
    dma = pltpu.SemaphoreType.DMA
    vmem = pl.BlockSpec(memory_space=pltpu.VMEM)
    smem = pl.BlockSpec(memory_space=pltpu.SMEM)
    hbm = pl.BlockSpec(memory_space=pl.ANY)
    return pl.pallas_call(
        functools.partial(kernel, n_store, n_mod, width),
        out_shape=jax.ShapeDtypeStruct((owned, samples), f32),
        in_specs=[vmem, smem, smem, hbm, hbm],
        out_specs=vmem,
        scratch_shapes=[
            pltpu.VMEM(fisher_inv.shape, bf16),
            pltpu.VMEM(stored_grads.shape, bf16),
            pltpu.VMEM(to_send.shape, bf16),
            pltpu.VMEM((n_store, rows, depth), bf16),
            pltpu.VMEM((chips, n_chunks, owned, width), f32),
            pltpu.VMEM((chips, n_chunks, owned, width), bf16),
            pltpu.VMEM((chips, n_chunks, owned, width), bf16),
            pltpu.VMEM((chips, n_chunks, owned, width), bf16),
            pltpu.VMEM((chips, n_chunks, owned, width), bf16),
            dma, dma((n_chunks,)),
            dma((n_mod,)), dma((n_mod,)),
            dma((n_store,)), dma((n_store,)),
            dma((chips, n_chunks)), dma((chips, n_chunks)),
            dma((chips, n_chunks)), dma((chips, n_chunks)),
        ],
        compiler_params=pltpu.CompilerParams(
            collective_id=0, has_side_effects=True, vmem_limit_bytes=56 * 1024 * 1024
        ),
        cost_estimate=pl.CostEstimate(
            flops=2 * queries * samples * depth, bytes_accessed=2 * samples * depth, transcendentals=0
        ),
        name="attribution",
    )(to_send, layer_of, layer_weight, fisher_inv, stored_grads)


def solution(mesh):
    in_specs = (
        P(("store", "mod"), None, None),
        P(("store", "mod"), None, None),
        P(("store", "mod"), None),
        P("mod"),
        P(),
        P("mod", None, None),
        P("store", "mod"),
    )
    out_specs = P("mod", "store")
    body = functools.partial(local, mesh.shape["store"], mesh.shape["mod"])
    return jax.shard_map(body, mesh=mesh, in_specs=in_specs, out_specs=out_specs, check_vma=False)
```

```python
import functools

import jax
import jax.numpy as jnp
from jax import lax
from jax.experimental import pallas as pl
from jax.experimental.pallas import tpu as pltpu
from jax.sharding import PartitionSpec as P

R = 32
LANES = 128
MESH = pl.DeviceIdType.MESH


def peer(index, step, count):
    if count & (count - 1):
        return lax.rem(index + step, count)
    other, bit = 0, 1
    while bit < count:
        other = other + ((index // bit + step // bit) % 2) * bit
        bit *= 2
    return other


def kernel(
    n_store, n_mod, width,
    act_hbm, grad_hbm, mask_ref, layer_ref, weight_ref, fisher_hbm, stored_hbm, out_ref,
    act, grad, outer, send_ref, act_sem, grad_sem,
    fisher, stored, blocks, everyone, keep, pair_out, pair_in, far_out, far_in,
    fisher_sem, stored_sem, block_send, block_recv, all_send, all_recv,
    pair_send, pair_recv, far_send, far_recv,
):
    s, k = lax.axis_index("store"), lax.axis_index("mod")
    chips = n_mod // 2
    chip, core = k // 2, k % 2
    sibling = k + 1 - 2 * core
    mods, entries = fisher.shape[0], fisher.shape[1]
    owned = out_ref.shape[0]
    samples = stored.shape[0]
    n_chunks = samples // width
    rows = everyone.shape[1]
    q_local = mask_ref.shape[0]

    def side_copies(g):
        lanes = pl.ds(pl.multiple_of(g * LANES, LANES), LANES)
        return (
            pltpu.make_async_copy(act_hbm.at[:, :, lanes], act.at[g], act_sem.at[g]),
            pltpu.make_async_copy(grad_hbm.at[:, :, lanes], grad.at[g], grad_sem.at[g]),
        )

    def group_at(step):
        return peer(chip, chips - 1 - step, chips)

    for step in range(chips):
        for copy in side_copies(group_at(step)):
            copy.start()
    barrier = pltpu.get_barrier_semaphore()
    for d in range(1, n_mod):
        pl.semaphore_signal(barrier, inc=1, device_id=(s, peer(k, d, n_mod)), device_id_type=MESH)
    for d in range(1, n_store):
        pl.semaphore_signal(barrier, inc=1, device_id=(peer(s, d, n_store), k), device_id_type=MESH)

    fisher_copy = pltpu.make_async_copy(fisher_hbm, fisher, fisher_sem)

    def stored_copy(c):
        part = pl.ds(pl.multiple_of(c * width, width), width)
        return pltpu.make_async_copy(stored_hbm.at[part, :], stored.at[part, :], stored_sem.at[c])

    def block_copy(to):
        return pltpu.make_async_remote_copy(
            src_ref=send_ref.at[to], dst_ref=blocks.at[k],
            send_sem=block_send.at[to], recv_sem=block_recv.at[k],
            device_id=(s, to), device_id_type=MESH,
        )

    quarter = lax.broadcasted_iota(jnp.int32, (q_local, LANES), 1) // R
    per_group = LANES // R

    def outer_step(step, carry):
        g = group_at(step)
        for copy in side_copies(g):
            copy.wait()

        @pl.when(step == 0)
        def _():
            fisher_copy.start()
            for c in range(n_chunks):
                stored_copy(c).start()

        for q in range(q_local):
            valid = mask_ref[q:q + 1, :].astype(jnp.float32)
            turned = (grad[g, q].astype(jnp.float32).T * valid).astype(jnp.bfloat16)
            outer[q * LANES:(q + 1) * LANES, :] = jnp.dot(
                turned, act[g, q], preferred_element_type=jnp.float32
            )

        def flat(a, part):
            row = None
            for r in range(per_group):
                line = outer[pl.ds(a * R + part * per_group + r, q_local, stride=LANES), :]
                shift = (R * (r - a)) % LANES
                if shift:
                    line = pltpu.roll(line, shift, 1)
                row = line if row is None else jnp.where(quarter == r, line, row)
            return row

        for half in range(2):
            for part in range(entries // LANES):
                lines = [flat(half * mods + m, part) for m in range(mods)]
                send_ref[2 * g + half, :, part * LANES:(part + 1) * LANES] = jnp.concatenate(
                    lines, axis=0
                ).astype(jnp.bfloat16)

        @pl.when(step == 0)
        def _():
            pl.semaphore_wait(barrier, n_mod + n_store - 2)

        for half in range(2):
            @pl.when(2 * g + half != k)
            def _():
                block_copy(2 * g + half).start()

        return carry

    lax.fori_loop(0, chips, outer_step, 0)
    blocks[k] = send_ref[k]
    fisher_copy.wait()
    for d in range(1, n_mod):
        source = peer(k, d, n_mod)
        pltpu.make_async_remote_copy(
            src_ref=send_ref.at[source], dst_ref=blocks.at[source],
            send_sem=block_send.at[source], recv_sem=block_recv.at[source],
            device_id=(s, source), device_id_type=MESH,
        ).wait_recv()

    arrived = blocks[...].astype(jnp.float32).reshape(n_mod, mods, q_local, entries)
    for m in range(mods):
        layer = layer_ref[m]
        scale = jnp.float32(0.0)
        for at in range(weight_ref.shape[0]):
            scale = scale + jnp.where(layer == at, weight_ref[at], jnp.float32(0.0))
        mine = arrived[:, m].reshape(n_mod * q_local, entries).astype(jnp.bfloat16)
        product = jnp.dot(mine, fisher[m], preferred_element_type=jnp.float32)
        everyone[s, :, m * entries:(m + 1) * entries] = (product * scale).astype(jnp.bfloat16)

    all_copies = []
    for d in range(1, n_store):
        to = peer(s, d, n_store)
        copy = pltpu.make_async_remote_copy(
            src_ref=everyone.at[s], dst_ref=everyone.at[s],
            send_sem=all_send.at[to], recv_sem=all_recv.at[s],
            device_id=(to, k), device_id_type=MESH,
        )
        copy.start()
        all_copies.append(copy)

    def span(c):
        return pl.ds(pl.multiple_of(c * width, width), width)

    def pair_copy(j, c):
        return pltpu.make_async_remote_copy(
            src_ref=pair_out.at[j, c], dst_ref=pair_in.at[j, c],
            send_sem=pair_send.at[j, c], recv_sem=pair_recv.at[j, c],
            device_id=(s, sibling), device_id_type=MESH,
        )

    def far_copy(j, c):
        return pltpu.make_async_remote_copy(
            src_ref=far_out.at[j, c], dst_ref=far_in.at[chip, c],
            send_sem=far_send.at[j, c], recv_sem=far_recv.at[chip, c],
            device_id=(s, 2 * j + core), device_id_type=MESH,
        )

    def far_arrival(source, c):
        return pltpu.make_async_remote_copy(
            src_ref=far_out.at[source, c], dst_ref=far_in.at[source, c],
            send_sem=far_send.at[source, c], recv_sem=far_recv.at[source, c],
            device_id=(s, 2 * source + core), device_id_type=MESH,
        )

    def finish_pair(step):
        j, c = peer(s, step // n_chunks, n_store), step % n_chunks
        pair_copy(j, c).wait_recv()
        total = keep[step % 2] + pair_in[j, c].astype(jnp.float32)

        @pl.when(j == chip)
        def _():
            out_ref[:, span(c)] = total

        @pl.when(j != chip)
        def _():
            far_out[j, c] = total.astype(jnp.bfloat16)
            far_copy(j, c).start()

    def score_step(step, carry):
        t, c = step // n_chunks, step % n_chunks
        j = peer(s, t, n_store)

        @pl.when((c == 0) & (t > 0))
        def _():
            pltpu.make_async_remote_copy(
                src_ref=everyone.at[j], dst_ref=everyone.at[j],
                send_sem=all_send.at[j], recv_sem=all_recv.at[j],
                device_id=(j, k), device_id_type=MESH,
            ).wait_recv()

        @pl.when(t == 0)
        def _():
            stored_copy(c).wait()

        part = lax.dot_general(
            everyone[j], stored[span(c), :], (((1,), (1,)), ((), ())), preferred_element_type=jnp.float32
        )
        low, high = part[:owned], part[owned:]
        first = core == 0
        keep[step % 2] = jnp.where(first, low, high)
        pair_out[j, c] = jnp.where(first, high, low).astype(jnp.bfloat16)
        pair_copy(j, c).start()

        @pl.when(step > 0)
        def _():
            finish_pair(step - 1)

        return carry

    steps = n_store * n_chunks
    lax.fori_loop(0, steps, score_step, 0)
    finish_pair(steps - 1)

    for d in range(1, chips):
        source = peer(chip, d, chips)
        for c in range(n_chunks):
            far_arrival(source, c).wait_recv()
            out_ref[:, c * width:(c + 1) * width] += far_in[source, c].astype(jnp.float32)

    for d in range(1, n_mod):
        block_copy(peer(k, d, n_mod)).wait_send()
    for copy in all_copies:
        copy.wait_send()
    for j in range(chips):
        for c in range(n_chunks):
            pair_copy(j, c).wait_send()

            @pl.when(j != chip)
            def _():
                far_copy(j, c).wait_send()


def local(n_store, n_mod, act_proj, grad_proj, token_mask, layer_of, layer_weight, fisher_inv, stored_grads):
    q_local, length, columns = act_proj.shape
    mods, entries = fisher_inv.shape[0], fisher_inv.shape[1]
    samples, depth = stored_grads.shape
    queries = q_local * n_store * n_mod
    owned, rows, chips = queries // n_mod, queries // n_store, n_mod // 2
    assert rows == 2 * owned and chips == n_store and columns == chips * LANES and 2 * mods * R == LANES
    width = min(1024, samples)
    n_chunks = samples // width
    bf16, f32 = jnp.bfloat16, jnp.float32
    dma = pltpu.SemaphoreType.DMA
    vmem = pl.BlockSpec(memory_space=pltpu.VMEM)
    smem = pl.BlockSpec(memory_space=pltpu.SMEM)
    hbm = pl.BlockSpec(memory_space=pl.ANY)
    return pl.pallas_call(
        functools.partial(kernel, n_store, n_mod, width),
        out_shape=jax.ShapeDtypeStruct((owned, samples), f32),
        in_specs=[hbm, hbm, vmem, smem, smem, hbm, hbm],
        out_specs=vmem,
        scratch_shapes=[
            pltpu.VMEM((chips, q_local, length, LANES), bf16),
            pltpu.VMEM((chips, q_local, length, LANES), bf16),
            pltpu.VMEM((q_local * LANES, LANES), f32),
            pltpu.VMEM((n_mod, mods * q_local, entries), bf16),
            dma((chips,)), dma((chips,)),
            pltpu.VMEM(fisher_inv.shape, bf16),
            pltpu.VMEM(stored_grads.shape, bf16),
            pltpu.VMEM((n_mod, mods * q_local, entries), bf16),
            pltpu.VMEM((n_store, rows, depth), bf16),
            pltpu.VMEM((2, owned, width), f32),
            pltpu.VMEM((chips, n_chunks, owned, width), bf16),
            pltpu.VMEM((chips, n_chunks, owned, width), bf16),
            pltpu.VMEM((chips, n_chunks, owned, width), bf16),
            pltpu.VMEM((chips, n_chunks, owned, width), bf16),
            dma, dma((n_chunks,)),
            dma((n_mod,)), dma((n_mod,)),
            dma((n_store,)), dma((n_store,)),
            dma((chips, n_chunks)), dma((chips, n_chunks)),
            dma((chips, n_chunks)), dma((chips, n_chunks)),
        ],
        compiler_params=pltpu.CompilerParams(
            collective_id=0, has_side_effects=True, vmem_limit_bytes=56 * 1024 * 1024
        ),
        cost_estimate=pl.CostEstimate(
            flops=2 * queries * samples * depth, bytes_accessed=2 * samples * depth, transcendentals=0
        ),
        name="attribution",
    )(act_proj, grad_proj, token_mask, layer_of, layer_weight, fisher_inv, stored_grads)


def solution(mesh):
    in_specs = (
        P(("store", "mod"), None, None),
        P(("store", "mod"), None, None),
        P(("store", "mod"), None),
        P("mod"),
        P(),
        P("mod", None, None),
        P("store", "mod"),
    )
    out_specs = P("mod", "store")
    body = functools.partial(local, mesh.shape["store"], mesh.shape["mod"])
    return jax.shard_map(body, mesh=mesh, in_specs=in_specs, out_specs=out_specs, check_vma=False)
```

```python
import functools

import jax
import jax.numpy as jnp
from jax import lax
from jax.experimental import pallas as pl
from jax.experimental.pallas import tpu as pltpu
from jax.sharding import PartitionSpec as P

R = 32
LANES = 128
HOP = 2
MESH = pl.DeviceIdType.MESH


def peer(index, step, count):
    if count & (count - 1):
        return lax.rem(index + step, count)
    other, bit = 0, 1
    while bit < count:
        other = other + ((index // bit + step // bit) % 2) * bit
        bit *= 2
    return other


def turn(step, count):
    if count & (count - 1) or count < 4:
        return step
    half = count // 2
    return (step % 2) * half + step // 2


def kernel(
    n_store, n_mod, width,
    act_hbm, grad_hbm, mask_ref, layer_ref, weight_ref, fisher_hbm, stored_hbm, out_ref,
    act, grad, outer, send_ref, act_sem, grad_sem,
    fisher, stored, blocks, everyone, keep, pair_out, pair_in, far_out, far_in,
    fisher_sem, stored_sem, block_send, block_recv, all_send, all_recv,
    pair_send, pair_recv, far_send, far_recv,
):
    s, k = lax.axis_index("store"), lax.axis_index("mod")
    chips = n_mod // 2
    chip, core = k // 2, k % 2
    sibling = k + 1 - 2 * core
    mods, entries = fisher.shape[0], fisher.shape[1]
    owned = out_ref.shape[0]
    samples = stored.shape[0]
    n_chunks = samples // width
    rows = everyone.shape[1]
    q_local = mask_ref.shape[0]

    def side_copies(g):
        lanes = pl.ds(pl.multiple_of(g * LANES, LANES), LANES)
        return (
            pltpu.make_async_copy(act_hbm.at[:, :, lanes], act.at[g], act_sem.at[g]),
            pltpu.make_async_copy(grad_hbm.at[:, :, lanes], grad.at[g], grad_sem.at[g]),
        )

    def group_at(step):
        return peer(chip, chips - 1 - step, chips)

    for step in range(chips):
        for copy in side_copies(group_at(step)):
            copy.start()
    barrier = pltpu.get_barrier_semaphore()
    for d in range(1, n_mod):
        pl.semaphore_signal(barrier, inc=1, device_id=(s, peer(k, d, n_mod)), device_id_type=MESH)
    for d in range(1, n_store):
        pl.semaphore_signal(barrier, inc=1, device_id=(peer(s, d, n_store), k), device_id_type=MESH)

    fisher_copy = pltpu.make_async_copy(fisher_hbm, fisher, fisher_sem)

    def stored_copy(c):
        part = pl.ds(pl.multiple_of(c * width, width), width)
        return pltpu.make_async_copy(stored_hbm.at[part, :], stored.at[part, :], stored_sem.at[c])

    def block_copy(to):
        return pltpu.make_async_remote_copy(
            src_ref=send_ref.at[to], dst_ref=blocks.at[k],
            send_sem=block_send.at[to], recv_sem=block_recv.at[k],
            device_id=(s, to), device_id_type=MESH,
        )

    quarter = lax.broadcasted_iota(jnp.int32, (q_local, LANES), 1) // R
    per_group = LANES // R

    def outer_step(step, carry):
        g = group_at(step)
        for copy in side_copies(g):
            copy.wait()

        @pl.when(step == 0)
        def _():
            fisher_copy.start()
            for c in range(n_chunks):
                stored_copy(c).start()

        for q in range(q_local):
            valid = mask_ref[q:q + 1, :].astype(jnp.float32)
            turned = (grad[g, q].astype(jnp.float32).T * valid).astype(jnp.bfloat16)
            outer[q * LANES:(q + 1) * LANES, :] = jnp.dot(
                turned, act[g, q], preferred_element_type=jnp.float32
            )

        def flat(a, part):
            row = None
            for r in range(per_group):
                line = outer[pl.ds(a * R + part * per_group + r, q_local, stride=LANES), :]
                shift = (R * (r - a)) % LANES
                if shift:
                    line = pltpu.roll(line, shift, 1)
                row = line if row is None else jnp.where(quarter == r, line, row)
            return row

        for half in range(2):
            for part in range(entries // LANES):
                lines = [flat(half * mods + m, part) for m in range(mods)]
                send_ref[2 * g + half, :, part * LANES:(part + 1) * LANES] = jnp.concatenate(
                    lines, axis=0
                ).astype(jnp.bfloat16)

        @pl.when(step == 0)
        def _():
            pl.semaphore_wait(barrier, n_mod + n_store - 2)

        for half in range(2):
            @pl.when(2 * g + half != k)
            def _():
                block_copy(2 * g + half).start()

        return carry

    lax.fori_loop(0, chips, outer_step, 0)
    blocks[k] = send_ref[k]
    fisher_copy.wait()
    for d in range(1, n_mod):
        source = peer(k, d, n_mod)
        pltpu.make_async_remote_copy(
            src_ref=send_ref.at[source], dst_ref=blocks.at[source],
            send_sem=block_send.at[source], recv_sem=block_recv.at[source],
            device_id=(s, source), device_id_type=MESH,
        ).wait_recv()

    def gather_copy(to, origin, m):
        part = everyone.at[origin, :, m * entries:(m + 1) * entries]
        return pltpu.make_async_remote_copy(
            src_ref=part, dst_ref=part,
            send_sem=all_send.at[to, m], recv_sem=all_recv.at[origin, m],
            device_id=(to, k), device_id_type=MESH,
        )

    arrived = blocks[...].astype(jnp.float32).reshape(n_mod, mods, q_local, entries)
    for m in range(mods):
        layer = layer_ref[m]
        scale = jnp.float32(0.0)
        for at in range(weight_ref.shape[0]):
            scale = scale + jnp.where(layer == at, weight_ref[at], jnp.float32(0.0))
        mine = arrived[:, m].reshape(n_mod * q_local, entries).astype(jnp.bfloat16)
        product = jnp.dot(mine, fisher[m], preferred_element_type=jnp.float32)
        everyone[s, :, m * entries:(m + 1) * entries] = (product * scale).astype(jnp.bfloat16)
        for d in range(1, n_store):
            gather_copy(peer(s, turn(d, n_store), n_store), s, m).start()

    def span(c):
        return pl.ds(pl.multiple_of(c * width, width), width)

    def pair_copy(j, c):
        return pltpu.make_async_remote_copy(
            src_ref=pair_out.at[j, c], dst_ref=pair_in.at[j, c],
            send_sem=pair_send.at[j, c], recv_sem=pair_recv.at[j, c],
            device_id=(s, sibling), device_id_type=MESH,
        )

    def far_copy(j, c):
        up = j > chip
        to = jnp.where(up, chip + 1, chip - 1)
        slot = jnp.where(up | (to != j), j, chips)
        return pltpu.make_async_remote_copy(
            src_ref=far_out.at[j, c], dst_ref=far_in.at[slot, c],
            send_sem=far_send.at[j, c], recv_sem=far_recv.at[slot, c],
            device_id=(s, 2 * to + core), device_id_type=MESH,
        )

    def add_arrival(slot, c, kept):
        pltpu.make_async_remote_copy(
            src_ref=far_out.at[0, c], dst_ref=far_in.at[slot, c],
            send_sem=far_send.at[0, c], recv_sem=far_recv.at[slot, c],
            device_id=(s, sibling), device_id_type=MESH,
        ).wait_recv()
        keep[kept] += far_in[slot, c].astype(jnp.float32)

    def where_is(step):
        return peer(s, turn(step // n_chunks, n_store), n_store), step % n_chunks

    def finish(step):
        j, c = where_is(step)
        kept = step % keep.shape[0]
        pair_copy(j, c).wait_recv()
        keep[kept] += pair_in[j, c].astype(jnp.float32)

        @pl.when(((j >= chip) & (chip > 0)) | ((j < chip) & (chip < chips - 1)))
        def _():
            add_arrival(j, c, kept)

        @pl.when((j == chip) & (chip < chips - 1))
        def _():
            add_arrival(chips, c, kept)

        @pl.when(j == chip)
        def _():
            out_ref[:, span(c)] = keep[kept]

        @pl.when(j != chip)
        def _():
            far_out[j, c] = keep[kept].astype(jnp.bfloat16)
            far_copy(j, c).start()

    def score(step):
        t = step // n_chunks
        j, c = where_is(step)

        @pl.when((c == 0) & (t > 0))
        def _():
            for m in range(mods):
                gather_copy(j, j, m).wait_recv()

        @pl.when(t == 0)
        def _():
            stored_copy(c).wait()

        part = lax.dot_general(
            everyone[j], stored[span(c), :], (((1,), (1,)), ((), ())), preferred_element_type=jnp.float32
        )
        low, high = part[:owned], part[owned:]
        first = core == 0
        keep[step % keep.shape[0]] = jnp.where(first, low, high)
        pair_out[j, c] = jnp.where(first, high, low).astype(jnp.bfloat16)
        pair_copy(j, c).start()

    steps = n_store * n_chunks
    gap = n_chunks

    def turn_of_loop(i, carry):
        @pl.when((i < n_chunks) | ((i >= n_chunks + gap) & (i < steps + gap)))
        def _():
            score(jnp.where(i < n_chunks, i, i - gap))

        def finish_at(hops, inner):
            at = i - 1 - hops * HOP
            step = jnp.where(at < n_chunks, at, at - gap)
            j, _ = where_is(jnp.maximum(step, 0))
            depth = jnp.where(j > chip, chip, chips - 1 - chip)
            depth = jnp.where(j == chip, jnp.maximum(chip, chips - 1 - chip), depth)

            @pl.when((((at >= 0) & (at < n_chunks)) | ((at >= n_chunks + gap) & (at < steps + gap))) & (depth == hops))
            def _():
                finish(step)

            return inner

        lax.fori_loop(0, chips, finish_at, 0)
        return carry

    lax.fori_loop(0, steps + gap + 1 + (chips - 1) * HOP, turn_of_loop, 0)

    for d in range(1, n_mod):
        block_copy(peer(k, d, n_mod)).wait_send()
    for d in range(1, n_store):
        for m in range(mods):
            gather_copy(peer(s, d, n_store), s, m).wait_send()
    for j in range(chips):
        for c in range(n_chunks):
            pair_copy(j, c).wait_send()

            @pl.when(j != chip)
            def _():
                far_copy(j, c).wait_send()


def local(n_store, n_mod, act_proj, grad_proj, token_mask, layer_of, layer_weight, fisher_inv, stored_grads):
    q_local, length, columns = act_proj.shape
    mods, entries = fisher_inv.shape[0], fisher_inv.shape[1]
    samples, depth = stored_grads.shape
    queries = q_local * n_store * n_mod
    owned, rows, chips = queries // n_mod, queries // n_store, n_mod // 2
    assert rows == 2 * owned and chips == n_store and columns == chips * LANES and 2 * mods * R == LANES
    width = min(1024, samples)
    n_chunks = samples // width
    bf16, f32 = jnp.bfloat16, jnp.float32
    dma = pltpu.SemaphoreType.DMA
    vmem = pl.BlockSpec(memory_space=pltpu.VMEM)
    smem = pl.BlockSpec(memory_space=pltpu.SMEM)
    hbm = pl.BlockSpec(memory_space=pl.ANY)
    return pl.pallas_call(
        functools.partial(kernel, n_store, n_mod, width),
        out_shape=jax.ShapeDtypeStruct((owned, samples), f32),
        in_specs=[hbm, hbm, vmem, smem, smem, hbm, hbm],
        out_specs=vmem,
        scratch_shapes=[
            pltpu.VMEM((chips, q_local, length, LANES), bf16),
            pltpu.VMEM((chips, q_local, length, LANES), bf16),
            pltpu.VMEM((q_local * LANES, LANES), f32),
            pltpu.VMEM((n_mod, mods * q_local, entries), bf16),
            dma((chips,)), dma((chips,)),
            pltpu.VMEM(fisher_inv.shape, bf16),
            pltpu.VMEM(stored_grads.shape, bf16),
            pltpu.VMEM((n_mod, mods * q_local, entries), bf16),
            pltpu.VMEM((n_store, rows, depth), bf16),
            pltpu.VMEM((2 + (chips - 1) * HOP, owned, width), f32),
            pltpu.VMEM((chips, n_chunks, owned, width), bf16),
            pltpu.VMEM((chips, n_chunks, owned, width), bf16),
            pltpu.VMEM((chips, n_chunks, owned, width), bf16),
            pltpu.VMEM((chips + 1, n_chunks, owned, width), bf16),
            dma, dma((n_chunks,)),
            dma((n_mod,)), dma((n_mod,)),
            dma((n_store, mods)), dma((n_store, mods)),
            dma((chips, n_chunks)), dma((chips, n_chunks)),
            dma((chips, n_chunks)), dma((chips + 1, n_chunks)),
        ],
        compiler_params=pltpu.CompilerParams(
            collective_id=0, has_side_effects=True, vmem_limit_bytes=60 * 1024 * 1024
        ),
        cost_estimate=pl.CostEstimate(
            flops=2 * queries * samples * depth, bytes_accessed=2 * samples * depth, transcendentals=0
        ),
        name="attribution",
    )(act_proj, grad_proj, token_mask, layer_of, layer_weight, fisher_inv, stored_grads)


def solution(mesh):
    in_specs = (
        P(("store", "mod"), None, None),
        P(("store", "mod"), None, None),
        P(("store", "mod"), None),
        P("mod"),
        P(),
        P("mod", None, None),
        P("store", "mod"),
    )
    out_specs = P("mod", "store")
    body = functools.partial(local, mesh.shape["store"], mesh.shape["mod"])
    return jax.shard_map(body, mesh=mesh, in_specs=in_specs, out_specs=out_specs, check_vma=False)
```

```python
import functools

import jax
import jax.numpy as jnp
from jax import lax
from jax.experimental import pallas as pl
from jax.experimental.pallas import tpu as pltpu
from jax.sharding import PartitionSpec as P

R = 32
LANES = 128
MESH = pl.DeviceIdType.MESH


def peer(index, step, count):
    if count & (count - 1):
        return lax.rem(index + step, count)
    other, bit = 0, 1
    while bit < count:
        other = other + ((index // bit + step // bit) % 2) * bit
        bit *= 2
    return other


def kernel(
    n_store, n_mod, deep,
    act_hbm, grad_hbm, mask_ref, layer_ref, weight_ref, fisher_hbm, stored_hbm, out_ref,
    act, grad, outer, send_ref, act_sem, grad_sem,
    fisher, stored, blocks, everyone, raw, keep, pair_out, pair_in, far_out, far_in,
    fisher_sem, stored_sem, block_send, block_recv, all_send, all_recv,
    pair_send, pair_recv, far_send, far_recv,
):
    s, k = lax.axis_index("store"), lax.axis_index("mod")
    chips = n_mod // 2
    chip, core = k // 2, k % 2
    sibling = k + 1 - 2 * core
    mods, entries = fisher.shape[0], fisher.shape[1]
    owned = out_ref.shape[0]
    samples = stored.shape[0]
    per = LANES // owned
    width = per * deep
    n_chunks = samples // width
    rows = everyone.shape[1]
    q_local = mask_ref.shape[0]

    def side_copies(g):
        lanes = pl.ds(pl.multiple_of(g * LANES, LANES), LANES)
        return (
            pltpu.make_async_copy(act_hbm.at[:, :, lanes], act.at[g], act_sem.at[g]),
            pltpu.make_async_copy(grad_hbm.at[:, :, lanes], grad.at[g], grad_sem.at[g]),
        )

    def group_at(step):
        return peer(chip, chips - 1 - step, chips)

    for step in range(chips):
        for copy in side_copies(group_at(step)):
            copy.start()
    raw[...] = jnp.zeros_like(raw)
    barrier = pltpu.get_barrier_semaphore()
    for d in range(1, n_mod):
        pl.semaphore_signal(barrier, inc=1, device_id=(s, peer(k, d, n_mod)), device_id_type=MESH)
    for d in range(1, n_store):
        pl.semaphore_signal(barrier, inc=1, device_id=(peer(s, d, n_store), k), device_id_type=MESH)

    fisher_copy = pltpu.make_async_copy(fisher_hbm, fisher, fisher_sem)

    def stored_copy(c):
        part = pl.ds(pl.multiple_of(c * width, width), width)
        return pltpu.make_async_copy(stored_hbm.at[part, :], stored.at[part, :], stored_sem.at[c])

    def block_copy(to):
        return pltpu.make_async_remote_copy(
            src_ref=send_ref.at[to], dst_ref=blocks.at[k],
            send_sem=block_send.at[to], recv_sem=block_recv.at[k],
            device_id=(s, to), device_id_type=MESH,
        )

    quarter = lax.broadcasted_iota(jnp.int32, (q_local, LANES), 1) // R
    per_group = LANES // R

    def outer_step(step, carry):
        g = group_at(step)
        for copy in side_copies(g):
            copy.wait()

        @pl.when(step == 0)
        def _():
            fisher_copy.start()
            for c in range(n_chunks):
                stored_copy(c).start()

        for q in range(q_local):
            valid = mask_ref[q:q + 1, :].astype(jnp.float32)
            turned = (grad[g, q].astype(jnp.float32).T * valid).astype(jnp.bfloat16)
            outer[q * LANES:(q + 1) * LANES, :] = jnp.dot(
                turned, act[g, q], preferred_element_type=jnp.float32
            )

        def flat(a, part):
            row = None
            for r in range(per_group):
                line = outer[pl.ds(a * R + part * per_group + r, q_local, stride=LANES), :]
                shift = (R * (r - a)) % LANES
                if shift:
                    line = pltpu.roll(line, shift, 1)
                row = line if row is None else jnp.where(quarter == r, line, row)
            return row

        for half in range(2):
            for part in range(entries // LANES):
                lines = [flat(half * mods + m, part) for m in range(mods)]
                send_ref[2 * g + half, :, part * LANES:(part + 1) * LANES] = jnp.concatenate(
                    lines, axis=0
                ).astype(jnp.bfloat16)

        @pl.when(step == 0)
        def _():
            pl.semaphore_wait(barrier, n_mod + n_store - 2)

        for half in range(2):
            @pl.when(2 * g + half != k)
            def _():
                block_copy(2 * g + half).start()

        return carry

    lax.fori_loop(0, chips, outer_step, 0)
    blocks[k] = send_ref[k]
    fisher_copy.wait()
    for d in range(1, n_mod):
        source = peer(k, d, n_mod)
        pltpu.make_async_remote_copy(
            src_ref=send_ref.at[source], dst_ref=blocks.at[source],
            send_sem=block_send.at[source], recv_sem=block_recv.at[source],
            device_id=(s, source), device_id_type=MESH,
        ).wait_recv()

    def gather_copy(t, m):
        lanes = pl.ds(m * entries, entries)
        return pltpu.make_async_remote_copy(
            src_ref=everyone.at[0, :, lanes], dst_ref=everyone.at[t, :, lanes],
            send_sem=all_send.at[t, m], recv_sem=all_recv.at[t, m],
            device_id=(peer(s, t, n_store), k), device_id_type=MESH,
        )

    arrived = blocks[...].astype(jnp.float32).reshape(n_mod, mods, q_local, entries)
    for m in range(mods):
        layer = layer_ref[m]
        scale = jnp.float32(0.0)
        for at in range(weight_ref.shape[0]):
            scale = scale + jnp.where(layer == at, weight_ref[at], jnp.float32(0.0))
        mine = arrived[:, m].reshape(n_mod * q_local, entries).astype(jnp.bfloat16)
        product = jnp.dot(mine, fisher[m], preferred_element_type=jnp.float32)
        everyone[0, :, m * entries:(m + 1) * entries] = (product * scale).astype(jnp.bfloat16)
        for d in range(n_store - 1, 0, -1):
            gather_copy(d, m).start()

    def span(c):
        return pl.ds(pl.multiple_of(c * width, width), width)

    def pair_copy(j, c):
        return pltpu.make_async_remote_copy(
            src_ref=pair_out.at[j, c], dst_ref=pair_in.at[j, c],
            send_sem=pair_send.at[j, c], recv_sem=pair_recv.at[j, c],
            device_id=(s, sibling), device_id_type=MESH,
        )

    def far_copy(j, c):
        up = j > chip
        to = jnp.where(up, chip + 1, chip - 1)
        slot = jnp.where(up | (to != j), j, chips)
        return pltpu.make_async_remote_copy(
            src_ref=far_out.at[j, c], dst_ref=far_in.at[slot, c],
            send_sem=far_send.at[j, c], recv_sem=far_recv.at[slot, c],
            device_id=(s, 2 * to + core), device_id_type=MESH,
        )

    def add_arrival(j, slot, c):
        pltpu.make_async_remote_copy(
            src_ref=far_out.at[0, c], dst_ref=far_in.at[slot, c],
            send_sem=far_send.at[0, c], recv_sem=far_recv.at[slot, c],
            device_id=(s, sibling), device_id_type=MESH,
        ).wait_recv()
        keep[j, c] += far_in[slot, c].astype(jnp.float32)

    def finish(j, c):
        pair_copy(j, c).wait_recv()
        keep[j, c] += pair_in[j, c].astype(jnp.float32)

        @pl.when(((j >= chip) & (chip > 0)) | ((j < chip) & (chip < chips - 1)))
        def _():
            add_arrival(j, j, c)

        @pl.when((j == chip) & (chip < chips - 1))
        def _():
            add_arrival(j, chips, c)

        @pl.when(j == chip)
        def _():
            turned = keep[j, c].T
            for a in range(per):
                lanes = pl.ds(pl.multiple_of(c * width + a * deep, LANES), deep)
                out_ref[:, lanes] = turned[a * owned:(a + 1) * owned]

        @pl.when(j != chip)
        def _():
            far_out[j, c] = keep[j, c].astype(jnp.bfloat16)
            far_copy(j, c).start()

    part_of_lane = lax.broadcasted_iota(jnp.int32, (deep, LANES), 1) // owned

    def side_by_side(at):
        column, offset = at // LANES * LANES, at % LANES
        block = None
        for a in range(per):
            piece = raw[a * deep:(a + 1) * deep, column:column + LANES]
            shift = (a * owned - offset) % LANES
            if shift:
                piece = pltpu.roll(piece, shift, 1)
            block = piece if block is None else jnp.where(part_of_lane == a, piece, block)
        return block

    def pair_off(j, c, at):
        low, high = side_by_side(at), side_by_side(at + owned)
        first = core == 0
        keep[j, c] = jnp.where(first, low, high)
        pair_out[j, c] = jnp.where(first, high, low).astype(jnp.bfloat16)
        pair_copy(j, c).start()

    def scores(queries, c):
        raw[:, :queries.shape[0]] = lax.dot_general(
            stored[span(c), :], queries, (((1,), (1,)), ((), ())), preferred_element_type=jnp.float32
        )

    order = list(range(n_store - 1, 0, -1))
    second = n_chunks + chips - 1

    def turn_of_loop(i, carry):
        @pl.when(i < n_chunks)
        def _():
            stored_copy(i).wait()
            scores(everyone[0], i)
            pair_off(s, i, 0)

        @pl.when(i == second)
        def _():
            for t in order:
                for m in range(mods):
                    gather_copy(t, m).wait_recv()

        @pl.when((i >= second) & (i < second + n_chunks))
        def _():
            c = i - second
            scores(everyone[1:].reshape((n_store - 1) * rows, -1), c)
            for t in order:
                pair_off(peer(s, t, n_store), c, (t - 1) * rows)

        def finish_at(hops, inner):
            at = i - 1 - hops

            def item(j, c):
                depth = jnp.where(j > chip, chip, chips - 1 - chip)
                depth = jnp.where(j == chip, jnp.maximum(chip, chips - 1 - chip), depth)

                @pl.when(depth == hops)
                def _():
                    finish(j, c)

            @pl.when((at >= 0) & (at < n_chunks))
            def _():
                item(s, at)

            @pl.when((at >= second) & (at < second + n_chunks))
            def _():
                for t in order:
                    item(peer(s, t, n_store), at - second)

            return inner

        lax.fori_loop(0, chips, finish_at, 0)
        return carry

    lax.fori_loop(0, second + n_chunks + chips, turn_of_loop, 0)

    for d in range(1, n_mod):
        block_copy(peer(k, d, n_mod)).wait_send()
    for d in range(1, n_store):
        for m in range(mods):
            gather_copy(d, m).wait_send()
    for j in range(chips):
        for c in range(n_chunks):
            pair_copy(j, c).wait_send()

            @pl.when(j != chip)
            def _():
                far_copy(j, c).wait_send()


def local(n_store, n_mod, act_proj, grad_proj, token_mask, layer_of, layer_weight, fisher_inv, stored_grads):
    q_local, length, columns = act_proj.shape
    mods, entries = fisher_inv.shape[0], fisher_inv.shape[1]
    samples, depth = stored_grads.shape
    queries = q_local * n_store * n_mod
    owned, rows, chips = queries // n_mod, queries // n_store, n_mod // 2
    assert rows == 2 * owned and chips == n_store and columns == chips * LANES and 2 * mods * R == LANES
    assert n_store & (n_store - 1) == 0 and n_mod & (n_mod - 1) == 0 and LANES % owned == 0
    deep = 256
    n_chunks = samples // (deep * (LANES // owned))
    wide = -(-(n_store - 1) * rows // LANES) * LANES
    bf16, f32 = jnp.bfloat16, jnp.float32
    dma = pltpu.SemaphoreType.DMA
    vmem = pl.BlockSpec(memory_space=pltpu.VMEM)
    smem = pl.BlockSpec(memory_space=pltpu.SMEM)
    hbm = pl.BlockSpec(memory_space=pl.ANY)
    return pl.pallas_call(
        functools.partial(kernel, n_store, n_mod, deep),
        out_shape=jax.ShapeDtypeStruct((owned, samples), f32),
        in_specs=[hbm, hbm, vmem, smem, smem, hbm, hbm],
        out_specs=vmem,
        scratch_shapes=[
            pltpu.VMEM((chips, q_local, length, LANES), bf16),
            pltpu.VMEM((chips, q_local, length, LANES), bf16),
            pltpu.VMEM((q_local * LANES, LANES), f32),
            pltpu.VMEM((n_mod, mods * q_local, entries), bf16),
            dma((chips,)), dma((chips,)),
            pltpu.VMEM(fisher_inv.shape, bf16),
            pltpu.VMEM(stored_grads.shape, bf16),
            pltpu.VMEM((n_mod, mods * q_local, entries), bf16),
            pltpu.VMEM((n_store, rows, depth), bf16),
            pltpu.VMEM((deep * (LANES // owned), wide), f32),
            pltpu.VMEM((chips, n_chunks, deep, LANES), f32),
            pltpu.VMEM((chips, n_chunks, deep, LANES), bf16),
            pltpu.VMEM((chips, n_chunks, deep, LANES), bf16),
            pltpu.VMEM((chips, n_chunks, deep, LANES), bf16),
            pltpu.VMEM((chips + 1, n_chunks, deep, LANES), bf16),
            dma, dma((n_chunks,)),
            dma((n_mod,)), dma((n_mod,)),
            dma((n_store, mods)), dma((n_store, mods)),
            dma((chips, n_chunks)), dma((chips, n_chunks)),
            dma((chips, n_chunks)), dma((chips + 1, n_chunks)),
        ],
        compiler_params=pltpu.CompilerParams(
            collective_id=0, has_side_effects=True, vmem_limit_bytes=(56 if chips <= 4 else 63) * 1024 * 1024
        ),
        cost_estimate=pl.CostEstimate(
            flops=2 * queries * samples * depth, bytes_accessed=2 * samples * depth, transcendentals=0
        ),
        name="attribution",
    )(act_proj, grad_proj, token_mask, layer_of, layer_weight, fisher_inv, stored_grads)


def solution(mesh):
    in_specs = (
        P(("store", "mod"), None, None),
        P(("store", "mod"), None, None),
        P(("store", "mod"), None),
        P("mod"),
        P(),
        P("mod", None, None),
        P("store", "mod"),
    )
    out_specs = P("mod", "store")
    body = functools.partial(local, mesh.shape["store"], mesh.shape["mod"])
    return jax.shard_map(body, mesh=mesh, in_specs=in_specs, out_specs=out_specs, check_vma=False)
```

```python
import functools

import jax
import jax.numpy as jnp
from jax import lax
from jax.experimental import pallas as pl
from jax.experimental.pallas import tpu as pltpu
from jax.sharding import PartitionSpec as P

R = 32
LANES = 128
PARTS = 2
GAP = 2
MESH = pl.DeviceIdType.MESH


def peer(index, step, count):
    if count & (count - 1):
        return lax.rem(index + step, count)
    other, bit = 0, 1
    while bit < count:
        other = other + ((index // bit + step // bit) % 2) * bit
        bit *= 2
    return other


def kernel(
    n_store, n_mod, deep,
    act_hbm, grad_hbm, mask_ref, layer_ref, weight_ref, fisher_hbm, stored_hbm, out_ref,
    act, grad, outer, send_ref, act_sem, grad_sem,
    fisher, stored, blocks, everyone, raw, keep, pair_out, pair_in, far_out, far_in,
    fisher_sem, stored_sem, block_send, block_recv, all_send, all_recv,
    pair_send, pair_recv, far_send, far_recv,
):
    s, k = lax.axis_index("store"), lax.axis_index("mod")
    chips = n_mod // 2
    chip, core = k // 2, k % 2
    sibling = k + 1 - 2 * core
    mods, entries = fisher.shape[0], fisher.shape[1]
    owned = out_ref.shape[0]
    samples = stored.shape[0]
    owned = owned // PARTS
    per = LANES // owned
    width = per * deep
    n_chunks = samples // width
    rows = everyone.shape[2]
    q_local = mask_ref.shape[0]

    def side_copies(g):
        lanes = pl.ds(pl.multiple_of(g * LANES, LANES), LANES)
        return (
            pltpu.make_async_copy(act_hbm.at[:, :, lanes], act.at[g], act_sem.at[g]),
            pltpu.make_async_copy(grad_hbm.at[:, :, lanes], grad.at[g], grad_sem.at[g]),
        )

    def group_at(step):
        return peer(chip, chips - 1 - step, chips)

    for step in range(chips):
        for copy in side_copies(group_at(step)):
            copy.start()
    raw[...] = jnp.zeros_like(raw)
    barrier = pltpu.get_barrier_semaphore()
    for d in range(1, n_mod):
        pl.semaphore_signal(barrier, inc=1, device_id=(s, peer(k, d, n_mod)), device_id_type=MESH)
    for d in range(1, n_store):
        pl.semaphore_signal(barrier, inc=1, device_id=(peer(s, d, n_store), k), device_id_type=MESH)

    fisher_copy = pltpu.make_async_copy(fisher_hbm, fisher, fisher_sem)

    def stored_copy(c):
        part = pl.ds(pl.multiple_of(c * width, width), width)
        return pltpu.make_async_copy(stored_hbm.at[part, :], stored.at[part, :], stored_sem.at[c])

    def block_copy(to):
        return pltpu.make_async_remote_copy(
            src_ref=send_ref.at[to], dst_ref=blocks.at[k],
            send_sem=block_send.at[to], recv_sem=block_recv.at[k],
            device_id=(s, to), device_id_type=MESH,
        )

    quarter = lax.broadcasted_iota(jnp.int32, (q_local, LANES), 1) // R
    per_group = LANES // R

    def outer_step(step, carry):
        g = group_at(step)
        for copy in side_copies(g):
            copy.wait()

        @pl.when(step == 0)
        def _():
            fisher_copy.start()
            for c in range(n_chunks):
                stored_copy(c).start()

        for q in range(q_local):
            valid = mask_ref[q:q + 1, :].astype(jnp.float32)
            turned = (grad[g, q].astype(jnp.float32).T * valid).astype(jnp.bfloat16)
            outer[q * LANES:(q + 1) * LANES, :] = jnp.dot(
                turned, act[g, q], preferred_element_type=jnp.float32
            )

        def flat(a, part):
            row = None
            for r in range(per_group):
                line = outer[pl.ds(a * R + part * per_group + r, q_local, stride=LANES), :]
                shift = (R * (r - a)) % LANES
                if shift:
                    line = pltpu.roll(line, shift, 1)
                row = line if row is None else jnp.where(quarter == r, line, row)
            return row

        for half in range(2):
            for part in range(entries // LANES):
                lines = [flat(half * mods + m, part) for m in range(mods)]
                send_ref[2 * g + half, :, part * LANES:(part + 1) * LANES] = jnp.concatenate(
                    lines, axis=0
                ).astype(jnp.bfloat16)

        @pl.when(step == 0)
        def _():
            pl.semaphore_wait(barrier, n_mod + n_store - 2)

        for half in range(2):
            @pl.when(2 * g + half != k)
            def _():
                block_copy(2 * g + half).start()

        return carry

    lax.fori_loop(0, chips, outer_step, 0)
    blocks[k] = send_ref[k]
    fisher_copy.wait()
    def gather_copy(u, t, m):
        lanes = pl.ds(m * entries, entries)
        return pltpu.make_async_remote_copy(
            src_ref=everyone.at[u, 0, :, lanes], dst_ref=everyone.at[u, t, :, lanes],
            send_sem=all_send.at[u, t, m], recv_sem=all_recv.at[u, t, m],
            device_id=(peer(s, t, n_store), k), device_id_type=MESH,
        )

    for u in range(PARTS):
        sources = [h * chips + u * (chips // PARTS) + b for h in range(2) for b in range(chips // PARTS)]
        for source in sources:
            @pl.when(k != source)
            def _():
                pltpu.make_async_remote_copy(
                    src_ref=send_ref.at[source], dst_ref=blocks.at[source],
                    send_sem=block_send.at[source], recv_sem=block_recv.at[source],
                    device_id=(s, source), device_id_type=MESH,
                ).wait_recv()
        arrived = [blocks[source].astype(jnp.float32) for source in sources]
        for m in range(mods):
            layer = layer_ref[m]
            scale = jnp.float32(0.0)
            for at in range(weight_ref.shape[0]):
                scale = scale + jnp.where(layer == at, weight_ref[at], jnp.float32(0.0))
            mine = jnp.concatenate([one[m * q_local:(m + 1) * q_local] for one in arrived], axis=0)
            product = jnp.dot(mine.astype(jnp.bfloat16), fisher[m], preferred_element_type=jnp.float32)
            everyone[u, 0, :, m * entries:(m + 1) * entries] = (product * scale).astype(jnp.bfloat16)
            for t in range(n_store - 1, 0, -1):
                gather_copy(u, t, m).start()

    def span(c):
        return pl.ds(pl.multiple_of(c * width, width), width)

    def pair_copy(j, c):
        return pltpu.make_async_remote_copy(
            src_ref=pair_out.at[j, c], dst_ref=pair_in.at[j, c],
            send_sem=pair_send.at[j, c], recv_sem=pair_recv.at[j, c],
            device_id=(s, sibling), device_id_type=MESH,
        )

    def far_copy(j, c):
        up = j > chip
        to = jnp.where(up, chip + 1, chip - 1)
        slot = jnp.where(up | (to != j), j, chips)
        return pltpu.make_async_remote_copy(
            src_ref=far_out.at[j, c], dst_ref=far_in.at[slot, c],
            send_sem=far_send.at[j, c], recv_sem=far_recv.at[slot, c],
            device_id=(s, 2 * to + core), device_id_type=MESH,
        )

    def add_arrival(j, slot, c):
        pltpu.make_async_remote_copy(
            src_ref=far_out.at[0, c], dst_ref=far_in.at[slot, c],
            send_sem=far_send.at[0, c], recv_sem=far_recv.at[slot, c],
            device_id=(s, sibling), device_id_type=MESH,
        ).wait_recv()
        keep[j, c] += far_in[slot, c].astype(jnp.float32)

    def finish(j, c):
        pair_copy(j, c).wait_recv()
        keep[j, c] += pair_in[j, c].astype(jnp.float32)

        @pl.when(((j >= chip) & (chip > 0)) | ((j < chip) & (chip < chips - 1)))
        def _():
            add_arrival(j, j, c)

        @pl.when((j == chip) & (chip < chips - 1))
        def _():
            add_arrival(j, chips, c)

        @pl.when(j == chip)
        def _():
            turned = keep[j, c].T
            part = pl.ds(pl.multiple_of(c // n_chunks * owned, owned), owned)
            for a in range(per):
                lanes = pl.ds(pl.multiple_of(c % n_chunks * width + a * deep, LANES), deep)
                out_ref[part, lanes] = turned[a * owned:(a + 1) * owned]

        @pl.when(j != chip)
        def _():
            far_out[j, c] = keep[j, c].astype(jnp.bfloat16)
            far_copy(j, c).start()

    part_of_lane = lax.broadcasted_iota(jnp.int32, (deep, LANES), 1) // owned

    def side_by_side(at):
        column, offset = at // LANES * LANES, at % LANES
        block = None
        for a in range(per):
            piece = raw[a * deep:(a + 1) * deep, column:column + LANES]
            shift = (a * owned - offset) % LANES
            if shift:
                piece = pltpu.roll(piece, shift, 1)
            block = piece if block is None else jnp.where(part_of_lane == a, piece, block)
        return block

    def pair_off(j, c, at):
        low, high = side_by_side(at), side_by_side(at + owned)
        first = core == 0
        keep[j, c] = jnp.where(first, low, high)
        pair_out[j, c] = jnp.where(first, high, low).astype(jnp.bfloat16)
        pair_copy(j, c).start()

    order = list(range(n_store - 1, -1, -1))
    steps = PARTS * n_chunks
    every = n_chunks + GAP

    def turn_of_loop(i, carry):
        u, c = i // every, i % every

        @pl.when((c == 0) & (u < PARTS))
        def _():
            for t in range(1, n_store):
                for m in range(mods):
                    gather_copy(u, t, m).wait_recv()

        @pl.when((c < n_chunks) & (u == 0))
        def _():
            stored_copy(c).wait()

        @pl.when((c < n_chunks) & (u < PARTS))
        def _():
            queries = everyone[u].reshape(n_store * rows, -1)
            raw[:, :n_store * rows] = lax.dot_general(
                stored[span(c), :], queries, (((1,), (1,)), ((), ())), preferred_element_type=jnp.float32
            )
            for t in order:
                pair_off(peer(s, t, n_store), u * n_chunks + c, t * rows)

        def finish_at(hops, inner):
            at = i - 1 - hops
            v, c = at // every, at % every

            @pl.when((at >= 0) & (v < PARTS) & (c < n_chunks))
            def _():
                for t in order:
                    j = peer(s, t, n_store)
                    depth = jnp.where(j > chip, chip, chips - 1 - chip)
                    depth = jnp.where(j == chip, jnp.maximum(chip, chips - 1 - chip), depth)

                    @pl.when(depth == hops)
                    def _():
                        finish(j, v * n_chunks + c)

            return inner

        lax.fori_loop(0, chips, finish_at, 0)
        return carry

    lax.fori_loop(0, PARTS * every + chips, turn_of_loop, 0)

    for d in range(1, n_mod):
        block_copy(peer(k, d, n_mod)).wait_send()
    for d in range(1, n_store):
        for u in range(PARTS):
            for m in range(mods):
                gather_copy(u, d, m).wait_send()
    for j in range(chips):
        for c in range(steps):
            pair_copy(j, c).wait_send()

            @pl.when(j != chip)
            def _():
                far_copy(j, c).wait_send()


def local(n_store, n_mod, act_proj, grad_proj, token_mask, layer_of, layer_weight, fisher_inv, stored_grads):
    q_local, length, columns = act_proj.shape
    mods, entries = fisher_inv.shape[0], fisher_inv.shape[1]
    samples, depth = stored_grads.shape
    queries = q_local * n_store * n_mod
    owned, rows, chips = queries // n_mod, queries // n_store, n_mod // 2
    assert rows == 2 * owned and chips == n_store and columns == chips * LANES and 2 * mods * R == LANES
    assert n_store & (n_store - 1) == 0 and n_mod & (n_mod - 1) == 0 and LANES % owned == 0
    deep = 128
    per = LANES // (owned // PARTS)
    n_chunks = samples // (deep * per)
    steps = PARTS * n_chunks
    wide = -(-queries // PARTS // LANES) * LANES
    bf16, f32 = jnp.bfloat16, jnp.float32
    dma = pltpu.SemaphoreType.DMA
    vmem = pl.BlockSpec(memory_space=pltpu.VMEM)
    smem = pl.BlockSpec(memory_space=pltpu.SMEM)
    hbm = pl.BlockSpec(memory_space=pl.ANY)
    return pl.pallas_call(
        functools.partial(kernel, n_store, n_mod, deep),
        out_shape=jax.ShapeDtypeStruct((owned, samples), f32),
        in_specs=[hbm, hbm, vmem, smem, smem, hbm, hbm],
        out_specs=vmem,
        scratch_shapes=[
            pltpu.VMEM((chips, q_local, length, LANES), bf16),
            pltpu.VMEM((chips, q_local, length, LANES), bf16),
            pltpu.VMEM((q_local * LANES, LANES), f32),
            pltpu.VMEM((n_mod, mods * q_local, entries), bf16),
            dma((chips,)), dma((chips,)),
            pltpu.VMEM(fisher_inv.shape, bf16),
            pltpu.VMEM(stored_grads.shape, bf16),
            pltpu.VMEM((n_mod, mods * q_local, entries), bf16),
            pltpu.VMEM((PARTS, n_store, rows // PARTS, depth), bf16),
            pltpu.VMEM((deep * per, wide), f32),
            pltpu.VMEM((chips, steps, deep, LANES), f32),
            pltpu.VMEM((chips, steps, deep, LANES), bf16),
            pltpu.VMEM((chips, steps, deep, LANES), bf16),
            pltpu.VMEM((chips, steps, deep, LANES), bf16),
            pltpu.VMEM((chips + 1, steps, deep, LANES), bf16),
            dma, dma((n_chunks,)),
            dma((n_mod,)), dma((n_mod,)),
            dma((PARTS, n_store, mods)), dma((PARTS, n_store, mods)),
            dma((chips, steps)), dma((chips, steps)),
            dma((chips, steps)), dma((chips + 1, steps)),
        ],
        compiler_params=pltpu.CompilerParams(
            collective_id=0, has_side_effects=True, vmem_limit_bytes=(56 if chips <= 4 else 63) * 1024 * 1024
        ),
        cost_estimate=pl.CostEstimate(
            flops=2 * queries * samples * depth, bytes_accessed=2 * samples * depth, transcendentals=0
        ),
        name="attribution",
    )(act_proj, grad_proj, token_mask, layer_of, layer_weight, fisher_inv, stored_grads)


def solution(mesh):
    in_specs = (
        P(("store", "mod"), None, None),
        P(("store", "mod"), None, None),
        P(("store", "mod"), None),
        P("mod"),
        P(),
        P("mod", None, None),
        P("store", "mod"),
    )
    out_specs = P("mod", "store")
    body = functools.partial(local, mesh.shape["store"], mesh.shape["mod"])
    return jax.shard_map(body, mesh=mesh, in_specs=in_specs, out_specs=out_specs, check_vma=False)
```

```python
import functools

import jax
import jax.numpy as jnp
from jax import lax
from jax.experimental import pallas as pl
from jax.experimental.pallas import tpu as pltpu
from jax.sharding import PartitionSpec as P

R = 32
LANES = 128
MESH = pl.DeviceIdType.MESH


def peer(index, step, count):
    if count & (count - 1):
        return lax.rem(index + step, count)
    other, bit = 0, 1
    while bit < count:
        other = other + ((index // bit + step // bit) % 2) * bit
        bit *= 2
    return other


def kernel(
    n_store, n_mod, deep,
    act_hbm, grad_hbm, mask_ref, layer_ref, weight_ref, fisher_hbm, stored_hbm, out_ref,
    act, grad, outer, send_ref, act_sem, grad_sem,
    fisher, stored, blocks, everyone, raw, keep, pair_out, pair_in, far_out, far_in,
    fisher_sem, stored_sem, block_send, block_recv, all_send, all_recv,
    pair_send, pair_recv, far_send, far_recv,
):
    s, k = lax.axis_index("store"), lax.axis_index("mod")
    chips = n_mod // 2
    chip, core = k // 2, k % 2
    sibling = k + 1 - 2 * core
    mods, entries = fisher.shape[0], fisher.shape[1]
    owned = out_ref.shape[0]
    samples = stored.shape[0]
    per = LANES // owned
    width = per * deep
    n_chunks = samples // width
    rows = everyone.shape[1]
    q_local = mask_ref.shape[0]

    def side_copies(g):
        lanes = pl.ds(pl.multiple_of(g * LANES, LANES), LANES)
        return (
            pltpu.make_async_copy(act_hbm.at[:, :, lanes], act.at[g], act_sem.at[g]),
            pltpu.make_async_copy(grad_hbm.at[:, :, lanes], grad.at[g], grad_sem.at[g]),
        )

    def group_at(step):
        return peer(chip, chips - 1 - step, chips)

    for step in range(chips):
        for copy in side_copies(group_at(step)):
            copy.start()
    raw[...] = jnp.zeros_like(raw)
    barrier = pltpu.get_barrier_semaphore()
    for d in range(1, n_mod):
        pl.semaphore_signal(barrier, inc=1, device_id=(s, peer(k, d, n_mod)), device_id_type=MESH)
    for d in range(1, n_store):
        pl.semaphore_signal(barrier, inc=1, device_id=(peer(s, d, n_store), k), device_id_type=MESH)

    fisher_copy = pltpu.make_async_copy(fisher_hbm, fisher, fisher_sem)

    def stored_copy(c):
        part = pl.ds(pl.multiple_of(c * width, width), width)
        return pltpu.make_async_copy(stored_hbm.at[part, :], stored.at[part, :], stored_sem.at[c])

    def block_copy(to):
        return pltpu.make_async_remote_copy(
            src_ref=send_ref.at[to], dst_ref=blocks.at[k],
            send_sem=block_send.at[to], recv_sem=block_recv.at[k],
            device_id=(s, to), device_id_type=MESH,
        )

    quarter = lax.broadcasted_iota(jnp.int32, (q_local, LANES), 1) // R
    per_group = LANES // R

    def outer_step(step, carry):
        g = group_at(step)
        for copy in side_copies(g):
            copy.wait()

        @pl.when(step == 0)
        def _():
            fisher_copy.start()
            for c in range(n_chunks):
                stored_copy(c).start()

        for q in range(q_local):
            valid = mask_ref[q:q + 1, :].astype(jnp.float32)
            turned = (grad[g, q].astype(jnp.float32).T * valid).astype(jnp.bfloat16)
            outer[q * LANES:(q + 1) * LANES, :] = jnp.dot(
                turned, act[g, q], preferred_element_type=jnp.float32
            )

        def flat(a, part):
            row = None
            for r in range(per_group):
                line = outer[pl.ds(a * R + part * per_group + r, q_local, stride=LANES), :]
                shift = (R * (r - a)) % LANES
                if shift:
                    line = pltpu.roll(line, shift, 1)
                row = line if row is None else jnp.where(quarter == r, line, row)
            return row

        for half in range(2):
            for part in range(entries // LANES):
                lines = [flat(half * mods + m, part) for m in range(mods)]
                send_ref[2 * g + half, :, part * LANES:(part + 1) * LANES] = jnp.concatenate(
                    lines, axis=0
                ).astype(jnp.bfloat16)

        @pl.when(step == 0)
        def _():
            pl.semaphore_wait(barrier, n_mod + n_store - 2)

        for half in range(2):
            @pl.when(2 * g + half != k)
            def _():
                block_copy(2 * g + half).start()

        return carry

    lax.fori_loop(0, chips, outer_step, 0)
    blocks[k] = send_ref[k]
    fisher_copy.wait()
    for d in range(1, n_mod):
        source = peer(k, d, n_mod)
        pltpu.make_async_remote_copy(
            src_ref=send_ref.at[source], dst_ref=blocks.at[source],
            send_sem=block_send.at[source], recv_sem=block_recv.at[source],
            device_id=(s, source), device_id_type=MESH,
        ).wait_recv()

    def gather_copy(t, m):
        lanes = pl.ds(m * entries, entries)
        return pltpu.make_async_remote_copy(
            src_ref=everyone.at[0, :, lanes], dst_ref=everyone.at[t, :, lanes],
            send_sem=all_send.at[t, m], recv_sem=all_recv.at[t, m],
            device_id=(peer(s, t, n_store), k), device_id_type=MESH,
        )

    arrived = blocks[...].astype(jnp.float32).reshape(n_mod, mods, q_local, entries)
    for m in range(mods):
        layer = layer_ref[m]
        scale = jnp.float32(0.0)
        for at in range(weight_ref.shape[0]):
            scale = scale + jnp.where(layer == at, weight_ref[at], jnp.float32(0.0))
        mine = arrived[:, m].reshape(n_mod * q_local, entries).astype(jnp.bfloat16)
        product = jnp.dot(mine, fisher[m], preferred_element_type=jnp.float32)
        everyone[0, :, m * entries:(m + 1) * entries] = (product * scale).astype(jnp.bfloat16)
        for d in range(1, n_store):
            gather_copy(d, m).start()

    def span(c):
        return pl.ds(pl.multiple_of(c * width, width), width)

    def pair_copy(j, c):
        return pltpu.make_async_remote_copy(
            src_ref=pair_out.at[j, c], dst_ref=pair_in.at[j, c],
            send_sem=pair_send.at[j, c], recv_sem=pair_recv.at[j, c],
            device_id=(s, sibling), device_id_type=MESH,
        )

    def far_copy(j, c):
        return pltpu.make_async_remote_copy(
            src_ref=far_out.at[j, c], dst_ref=far_in.at[chip, c],
            send_sem=far_send.at[j, c], recv_sem=far_recv.at[chip, c],
            device_id=(s, 2 * j + core), device_id_type=MESH,
        )

    def finish(j, c):
        pair_copy(j, c).wait_recv()

        @pl.when(j == chip)
        def _():
            keep[j, c] += pair_in[j, c].astype(jnp.float32)

        @pl.when(j != chip)
        def _():
            far_out[j, c] = (keep[j, c] + pair_in[j, c].astype(jnp.float32)).astype(jnp.bfloat16)
            far_copy(j, c).start()

    part_of_lane = lax.broadcasted_iota(jnp.int32, (deep, LANES), 1) // owned

    def side_by_side(at):
        column, offset = at // LANES * LANES, at % LANES
        block = None
        for a in range(per):
            piece = raw[a * deep:(a + 1) * deep, column:column + LANES]
            shift = (a * owned - offset) % LANES
            if shift:
                piece = pltpu.roll(piece, shift, 1)
            block = piece if block is None else jnp.where(part_of_lane == a, piece, block)
        return block

    def pair_off(j, c, at):
        low, high = side_by_side(at), side_by_side(at + owned)
        first = core == 0
        keep[j, c] = jnp.where(first, low, high)
        pair_out[j, c] = jnp.where(first, high, low).astype(jnp.bfloat16)
        pair_copy(j, c).start()

    def scores(queries, c):
        raw[:, :queries.shape[0]] = lax.dot_general(
            stored[span(c), :], queries, (((1,), (1,)), ((), ())), preferred_element_type=jnp.float32
        )

    bounds = [0, 1, min(3, n_store), n_store]
    for first_t, end_t in zip(bounds[:-1], bounds[1:]):
        if first_t == end_t:
            continue
        if first_t:
            for t in range(first_t, end_t):
                for m in range(mods):
                    gather_copy(t, m).wait_recv()

        def step(c, carry, first_t=first_t, end_t=end_t):
            if first_t == 0:
                stored_copy(c).wait()
            scores(everyone[first_t:end_t].reshape((end_t - first_t) * rows, -1), c)
            for t in range(end_t - 1, first_t - 1, -1):
                pair_off(peer(s, t, n_store), c, (t - first_t) * rows)

            @pl.when(c > 0)
            def _():
                for t in range(end_t - 1, first_t - 1, -1):
                    finish(peer(s, t, n_store), c - 1)

            return carry

        lax.fori_loop(0, n_chunks, step, 0)
        for t in range(end_t - 1, first_t - 1, -1):
            finish(peer(s, t, n_store), n_chunks - 1)

    def own_sum(c, carry):
        total = keep[chip, c]
        for d in range(1, chips):
            source = peer(chip, d, chips)
            pltpu.make_async_remote_copy(
                src_ref=far_out.at[source, c], dst_ref=far_in.at[source, c],
                send_sem=far_send.at[source, c], recv_sem=far_recv.at[source, c],
                device_id=(s, 2 * source + core), device_id_type=MESH,
            ).wait_recv()
            total = total + far_in[source, c].astype(jnp.float32)
        turned = total.T
        for a in range(per):
            lanes = pl.ds(pl.multiple_of(c * width + a * deep, LANES), deep)
            out_ref[:, lanes] = turned[a * owned:(a + 1) * owned]
        return carry

    lax.fori_loop(0, n_chunks, own_sum, 0)

    for d in range(1, n_mod):
        block_copy(peer(k, d, n_mod)).wait_send()
    for d in range(1, n_store):
        for m in range(mods):
            gather_copy(d, m).wait_send()
    for j in range(chips):
        for c in range(n_chunks):
            pair_copy(j, c).wait_send()

            @pl.when(j != chip)
            def _():
                far_copy(j, c).wait_send()


def local(n_store, n_mod, act_proj, grad_proj, token_mask, layer_of, layer_weight, fisher_inv, stored_grads):
    q_local, length, columns = act_proj.shape
    mods, entries = fisher_inv.shape[0], fisher_inv.shape[1]
    samples, depth = stored_grads.shape
    queries = q_local * n_store * n_mod
    owned, rows, chips = queries // n_mod, queries // n_store, n_mod // 2
    assert rows == 2 * owned and chips == n_store and columns == chips * LANES and 2 * mods * R == LANES
    assert n_store & (n_store - 1) == 0 and n_mod & (n_mod - 1) == 0 and LANES % owned == 0
    deep = 256
    n_chunks = samples // (deep * (LANES // owned))
    wide = -(-(n_store - 1) * rows // LANES) * LANES
    bf16, f32 = jnp.bfloat16, jnp.float32
    dma = pltpu.SemaphoreType.DMA
    vmem = pl.BlockSpec(memory_space=pltpu.VMEM)
    smem = pl.BlockSpec(memory_space=pltpu.SMEM)
    hbm = pl.BlockSpec(memory_space=pl.ANY)
    return pl.pallas_call(
        functools.partial(kernel, n_store, n_mod, deep),
        out_shape=jax.ShapeDtypeStruct((owned, samples), f32),
        in_specs=[hbm, hbm, vmem, smem, smem, hbm, hbm],
        out_specs=vmem,
        scratch_shapes=[
            pltpu.VMEM((chips, q_local, length, LANES), bf16),
            pltpu.VMEM((chips, q_local, length, LANES), bf16),
            pltpu.VMEM((q_local * LANES, LANES), f32),
            pltpu.VMEM((n_mod, mods * q_local, entries), bf16),
            dma((chips,)), dma((chips,)),
            pltpu.VMEM(fisher_inv.shape, bf16),
            pltpu.VMEM(stored_grads.shape, bf16),
            pltpu.VMEM((n_mod, mods * q_local, entries), bf16),
            pltpu.VMEM((n_store, rows, depth), bf16),
            pltpu.VMEM((deep * (LANES // owned), wide), f32),
            pltpu.VMEM((chips, n_chunks, deep, LANES), f32),
            pltpu.VMEM((chips, n_chunks, deep, LANES), bf16),
            pltpu.VMEM((chips, n_chunks, deep, LANES), bf16),
            pltpu.VMEM((chips, n_chunks, deep, LANES), bf16),
            pltpu.VMEM((chips, n_chunks, deep, LANES), bf16),
            dma, dma((n_chunks,)),
            dma((n_mod,)), dma((n_mod,)),
            dma((n_store, mods)), dma((n_store, mods)),
            dma((chips, n_chunks)), dma((chips, n_chunks)),
            dma((chips, n_chunks)), dma((chips, n_chunks)),
        ],
        compiler_params=pltpu.CompilerParams(
            collective_id=0, has_side_effects=True, vmem_limit_bytes=(56 if chips <= 4 else 63) * 1024 * 1024
        ),
        cost_estimate=pl.CostEstimate(
            flops=2 * queries * samples * depth, bytes_accessed=2 * samples * depth, transcendentals=0
        ),
        name="attribution",
    )(act_proj, grad_proj, token_mask, layer_of, layer_weight, fisher_inv, stored_grads)


def solution(mesh):
    in_specs = (
        P(("store", "mod"), None, None),
        P(("store", "mod"), None, None),
        P(("store", "mod"), None),
        P("mod"),
        P(),
        P("mod", None, None),
        P("store", "mod"),
    )
    out_specs = P("mod", "store")
    body = functools.partial(local, mesh.shape["store"], mesh.shape["mod"])
    return jax.shard_map(body, mesh=mesh, in_specs=in_specs, out_specs=out_specs, check_vma=False)
```

```python
import functools

import jax
import jax.numpy as jnp
from jax import lax
from jax.experimental import pallas as pl
from jax.experimental.pallas import tpu as pltpu
from jax.sharding import PartitionSpec as P

R = 32
LANES = 128
MESH = pl.DeviceIdType.MESH


def peer(index, step, count):
    if count & (count - 1):
        return lax.rem(index + step, count)
    other, bit = 0, 1
    while bit < count:
        other = other + ((index // bit + step // bit) % 2) * bit
        bit *= 2
    return other


def kernel(
    n_store, n_mod, deep,
    act_hbm, grad_hbm, mask_ref, layer_ref, weight_ref, fisher_hbm, stored_hbm, out_ref,
    act, grad, outer, send_ref, act_sem, grad_sem,
    fisher, stored, blocks, everyone, raw, keep, pair_out, pair_in, far_out, far_in,
    fisher_sem, stored_sem, block_send, block_recv, all_send, all_recv,
    pair_send, pair_recv, far_send, far_recv,
):
    s, k = lax.axis_index("store"), lax.axis_index("mod")
    chips = n_mod // 2
    chip, core = k // 2, k % 2
    sibling = k + 1 - 2 * core
    mods, entries = fisher.shape[0], fisher.shape[1]
    owned = out_ref.shape[0]
    samples = stored.shape[0]
    per = LANES // owned
    width = per * deep
    n_chunks = samples // width
    rows = everyone.shape[1]
    q_local = mask_ref.shape[0]

    def side_copies(g):
        lanes = pl.ds(pl.multiple_of(g * LANES, LANES), LANES)
        return (
            pltpu.make_async_copy(act_hbm.at[:, :, lanes], act.at[g], act_sem.at[g]),
            pltpu.make_async_copy(grad_hbm.at[:, :, lanes], grad.at[g], grad_sem.at[g]),
        )

    def group_at(step):
        return peer(chip, chips - 1 - step, chips)

    for step in range(chips):
        for copy in side_copies(group_at(step)):
            copy.start()
    raw[...] = jnp.zeros_like(raw)
    barrier = pltpu.get_barrier_semaphore()
    for d in range(1, n_mod):
        pl.semaphore_signal(barrier, inc=1, device_id=(s, peer(k, d, n_mod)), device_id_type=MESH)
    for d in range(1, n_store):
        pl.semaphore_signal(barrier, inc=1, device_id=(peer(s, d, n_store), k), device_id_type=MESH)

    fisher_copy = pltpu.make_async_copy(fisher_hbm, fisher, fisher_sem)

    def stored_copy(c):
        part = pl.ds(pl.multiple_of(c * width, width), width)
        return pltpu.make_async_copy(stored_hbm.at[part, :], stored.at[part, :], stored_sem.at[c])

    def block_copy(to):
        return pltpu.make_async_remote_copy(
            src_ref=send_ref.at[to], dst_ref=blocks.at[k],
            send_sem=block_send.at[to], recv_sem=block_recv.at[k],
            device_id=(s, to), device_id_type=MESH,
        )

    quarter = lax.broadcasted_iota(jnp.int32, (q_local, LANES), 1) // R
    per_group = LANES // R

    def outer_step(step, carry):
        g = group_at(step)
        for copy in side_copies(g):
            copy.wait()

        @pl.when(step == 0)
        def _():
            fisher_copy.start()
            for c in range(n_chunks):
                stored_copy(c).start()

        for q in range(q_local):
            valid = mask_ref[q:q + 1, :].astype(jnp.bfloat16)
            turned = grad[g, q].T * valid
            outer[q * LANES:(q + 1) * LANES, :] = jnp.dot(
                turned, act[g, q], preferred_element_type=jnp.float32
            )

        def flat(a, part):
            row = None
            for r in range(per_group):
                line = outer[pl.ds(a * R + part * per_group + r, q_local, stride=LANES), :]
                shift = (R * (r - a)) % LANES
                if shift:
                    line = pltpu.roll(line, shift, 1)
                row = line if row is None else jnp.where(quarter == r, line, row)
            return row

        for half in range(2):
            for part in range(entries // LANES):
                lines = [flat(half * mods + m, part) for m in range(mods)]
                send_ref[2 * g + half, :, part * LANES:(part + 1) * LANES] = jnp.concatenate(
                    lines, axis=0
                ).astype(jnp.bfloat16)

        @pl.when(step == 0)
        def _():
            pl.semaphore_wait(barrier, n_mod + n_store - 2)

        for half in range(2):
            @pl.when(2 * g + half != k)
            def _():
                block_copy(2 * g + half).start()

        return carry

    lax.fori_loop(0, chips, outer_step, 0)
    blocks[k] = send_ref[k]
    fisher_copy.wait()
    for d in range(1, n_mod):
        source = peer(k, d, n_mod)
        pltpu.make_async_remote_copy(
            src_ref=send_ref.at[source], dst_ref=blocks.at[source],
            send_sem=block_send.at[source], recv_sem=block_recv.at[source],
            device_id=(s, source), device_id_type=MESH,
        ).wait_recv()

    def gather_copy(t, m):
        lanes = pl.ds(m * entries, entries)
        return pltpu.make_async_remote_copy(
            src_ref=everyone.at[0, :, lanes], dst_ref=everyone.at[t, :, lanes],
            send_sem=all_send.at[t, m], recv_sem=all_recv.at[t, m],
            device_id=(peer(s, t, n_store), k), device_id_type=MESH,
        )

    arrived = blocks[...].astype(jnp.float32).reshape(n_mod, mods, q_local, entries)
    for m in range(mods):
        layer = layer_ref[m]
        scale = jnp.float32(0.0)
        for at in range(weight_ref.shape[0]):
            scale = scale + jnp.where(layer == at, weight_ref[at], jnp.float32(0.0))
        mine = arrived[:, m].reshape(n_mod * q_local, entries).astype(jnp.bfloat16)
        product = jnp.dot(mine, fisher[m], preferred_element_type=jnp.float32)
        everyone[0, :, m * entries:(m + 1) * entries] = (product * scale).astype(jnp.bfloat16)
        for d in range(1, n_store):
            gather_copy(d, m).start()

    def span(c):
        return pl.ds(pl.multiple_of(c * width, width), width)

    def pair_copy(j, c):
        return pltpu.make_async_remote_copy(
            src_ref=pair_out.at[j, c], dst_ref=pair_in.at[j, c],
            send_sem=pair_send.at[j, c], recv_sem=pair_recv.at[j, c],
            device_id=(s, sibling), device_id_type=MESH,
        )

    def far_copy(j, c):
        return pltpu.make_async_remote_copy(
            src_ref=far_out.at[j, c], dst_ref=far_in.at[chip, c],
            send_sem=far_send.at[j, c], recv_sem=far_recv.at[chip, c],
            device_id=(s, 2 * j + core), device_id_type=MESH,
        )

    def finish(j, c):
        pair_copy(j, c).wait_recv()

        @pl.when(j == chip)
        def _():
            keep[j, c] += pair_in[j, c].astype(jnp.float32)

        @pl.when(j != chip)
        def _():
            far_out[j, c] = (keep[j, c] + pair_in[j, c].astype(jnp.float32)).astype(jnp.bfloat16)
            far_copy(j, c).start()

    part_of_lane = lax.broadcasted_iota(jnp.int32, (deep, LANES), 1) // owned

    def side_by_side(at):
        column, offset = at // LANES * LANES, at % LANES
        block = None
        for a in range(per):
            piece = raw[a * deep:(a + 1) * deep, column:column + LANES]
            shift = (a * owned - offset) % LANES
            if shift:
                piece = pltpu.roll(piece, shift, 1)
            block = piece if block is None else jnp.where(part_of_lane == a, piece, block)
        return block

    def pair_off(j, c, at):
        low, high = side_by_side(at), side_by_side(at + owned)
        first = core == 0
        keep[j, c] = jnp.where(first, low, high)
        pair_out[j, c] = jnp.where(first, high, low).astype(jnp.bfloat16)
        pair_copy(j, c).start()

    def scores(queries, c):
        raw[:, :queries.shape[0]] = lax.dot_general(
            stored[span(c), :], queries, (((1,), (1,)), ((), ())), preferred_element_type=jnp.float32
        )

    bounds = [0, 1, min(3, n_store), n_store]
    for first_t, end_t in zip(bounds[:-1], bounds[1:]):
        if first_t == end_t:
            continue
        if first_t:
            for t in range(first_t, end_t):
                for m in range(mods):
                    gather_copy(t, m).wait_recv()

        def step(c, carry, first_t=first_t, end_t=end_t):
            if first_t == 0:
                stored_copy(c).wait()
            scores(everyone[first_t:end_t].reshape((end_t - first_t) * rows, -1), c)
            for t in range(end_t - 1, first_t - 1, -1):
                pair_off(peer(s, t, n_store), c, (t - first_t) * rows)

            @pl.when(c > 0)
            def _():
                for t in range(end_t - 1, first_t - 1, -1):
                    finish(peer(s, t, n_store), c - 1)

            return carry

        lax.fori_loop(0, n_chunks, step, 0)
        for t in range(end_t - 1, first_t - 1, -1):
            finish(peer(s, t, n_store), n_chunks - 1)

    def own_sum(c, carry):
        total = keep[chip, c]
        for d in range(1, chips):
            source = peer(chip, d, chips)
            pltpu.make_async_remote_copy(
                src_ref=far_out.at[source, c], dst_ref=far_in.at[source, c],
                send_sem=far_send.at[source, c], recv_sem=far_recv.at[source, c],
                device_id=(s, 2 * source + core), device_id_type=MESH,
            ).wait_recv()
            total = total + far_in[source, c].astype(jnp.float32)
        turned = total.T
        for a in range(per):
            lanes = pl.ds(pl.multiple_of(c * width + a * deep, LANES), deep)
            out_ref[:, lanes] = turned[a * owned:(a + 1) * owned]
        return carry

    lax.fori_loop(0, n_chunks, own_sum, 0)

    for d in range(1, n_mod):
        block_copy(peer(k, d, n_mod)).wait_send()
    for d in range(1, n_store):
        for m in range(mods):
            gather_copy(d, m).wait_send()
    for j in range(chips):
        for c in range(n_chunks):
            pair_copy(j, c).wait_send()

            @pl.when(j != chip)
            def _():
                far_copy(j, c).wait_send()


def local(n_store, n_mod, act_proj, grad_proj, token_mask, layer_of, layer_weight, fisher_inv, stored_grads):
    q_local, length, columns = act_proj.shape
    mods, entries = fisher_inv.shape[0], fisher_inv.shape[1]
    samples, depth = stored_grads.shape
    queries = q_local * n_store * n_mod
    owned, rows, chips = queries // n_mod, queries // n_store, n_mod // 2
    assert rows == 2 * owned and chips == n_store and columns == chips * LANES and 2 * mods * R == LANES
    assert n_store & (n_store - 1) == 0 and n_mod & (n_mod - 1) == 0 and LANES % owned == 0
    deep = 256
    n_chunks = samples // (deep * (LANES // owned))
    wide = -(-(n_store - 1) * rows // LANES) * LANES
    bf16, f32 = jnp.bfloat16, jnp.float32
    dma = pltpu.SemaphoreType.DMA
    vmem = pl.BlockSpec(memory_space=pltpu.VMEM)
    smem = pl.BlockSpec(memory_space=pltpu.SMEM)
    hbm = pl.BlockSpec(memory_space=pl.ANY)
    return pl.pallas_call(
        functools.partial(kernel, n_store, n_mod, deep),
        out_shape=jax.ShapeDtypeStruct((owned, samples), f32),
        in_specs=[hbm, hbm, vmem, smem, smem, hbm, hbm],
        out_specs=vmem,
        scratch_shapes=[
            pltpu.VMEM((chips, q_local, length, LANES), bf16),
            pltpu.VMEM((chips, q_local, length, LANES), bf16),
            pltpu.VMEM((q_local * LANES, LANES), f32),
            pltpu.VMEM((n_mod, mods * q_local, entries), bf16),
            dma((chips,)), dma((chips,)),
            pltpu.VMEM(fisher_inv.shape, bf16),
            pltpu.VMEM(stored_grads.shape, bf16),
            pltpu.VMEM((n_mod, mods * q_local, entries), bf16),
            pltpu.VMEM((n_store, rows, depth), bf16),
            pltpu.VMEM((deep * (LANES // owned), wide), f32),
            pltpu.VMEM((chips, n_chunks, deep, LANES), f32),
            pltpu.VMEM((chips, n_chunks, deep, LANES), bf16),
            pltpu.VMEM((chips, n_chunks, deep, LANES), bf16),
            pltpu.VMEM((chips, n_chunks, deep, LANES), bf16),
            pltpu.VMEM((chips, n_chunks, deep, LANES), bf16),
            dma, dma((n_chunks,)),
            dma((n_mod,)), dma((n_mod,)),
            dma((n_store, mods)), dma((n_store, mods)),
            dma((chips, n_chunks)), dma((chips, n_chunks)),
            dma((chips, n_chunks)), dma((chips, n_chunks)),
        ],
        compiler_params=pltpu.CompilerParams(
            collective_id=0, has_side_effects=True, vmem_limit_bytes=(56 if chips <= 4 else 63) * 1024 * 1024
        ),
        cost_estimate=pl.CostEstimate(
            flops=2 * queries * samples * depth, bytes_accessed=2 * samples * depth, transcendentals=0
        ),
        name="attribution",
    )(act_proj, grad_proj, token_mask, layer_of, layer_weight, fisher_inv, stored_grads)


def solution(mesh):
    in_specs = (
        P(("store", "mod"), None, None),
        P(("store", "mod"), None, None),
        P(("store", "mod"), None),
        P("mod"),
        P(),
        P("mod", None, None),
        P("store", "mod"),
    )
    out_specs = P("mod", "store")
    body = functools.partial(local, mesh.shape["store"], mesh.shape["mod"])
    return jax.shard_map(body, mesh=mesh, in_specs=in_specs, out_specs=out_specs, check_vma=False)
```
